32 devices in a mesh: space: 8 (over z, y), dp: 4 (over x, core).
Axes of the slice: x: 2, y: 2, z: 4, core: 2. Of those that a mesh axis runs over, the one named last changes fastest.
Arguments:
- forcing: bfloat16 [4, 128, 16, 8, 128], P('dp', 'space'), may hold values from -6 to 6
- hidden_prev: bfloat16 [4, 128, 64, 8, 128], P('dp', 'space'), may hold values from -0.8984375 to 0.8984375
- cell_prev: bfloat16 [4, 128, 64, 8, 128], P('dp', 'space'), may hold values from -4 to 4
- hidden_grad: bfloat16 [4, 128, 64, 8, 128], P('dp', 'space'), may hold values from -0.0625 to 0.0625
- w_gates: bfloat16 [256, 720], replicated, may hold values from -0.21875 to 0.21875
- gate_bias: float32 [256], replicated, may hold values from -4 to 4
- worker: int32 [4, 128], P('dp'), may hold values from -1 to 7, as said below
Outputs:
- hidden_next: bfloat16 [4, 128, 64, 8, 128], P('dp', 'space')
- cell_next: bfloat16 [4, 128, 64, 8, 128], P('dp', 'space')
- weight_grad: float32 [256, 720], P('space')
- bias_grad: float32 [256], P('space')
The draws below stay inside these ranges and needn't reach their ends.
Inputs may be any that keep to these rules, and one draw needn't show every extreme that they name: Each year's active tiles (worker >= 0) are dealt to workers in increasing tile order: the j-th active tile, from 0, goes to worker j modulo the number of devices along space; every year has exactly 8 active tiles for every worker, one home in every year has all 16 of its tiles active, and so at most 2 tiles, reached, go from one home to one worker.
All inputs are finite; a program needn't handle non-finite values.
Results may differ from the reference program's by a relative error of at most 0.0075.
Values may be sent and summed in bfloat16 or wider, within the bound.
A program may use at most 64 MiB of HBM per device.

```python
import jax
import jax.numpy as jnp
from jax import lax

CIN = 16
HID = 64
TILE_ROWS = 8
TILE_COLS = 128
TW = 4
KIN = 80
GATES = 256
TH = 16
CAP = 8
TILES = 128
YEARS = 4


def draw_worker(key, part):
    homes = TILES // TH

    def one_year(year_key):
        key_order, key_count, key_pick = jax.random.split(year_key, 3)
        order = jax.random.permutation(key_order, homes)
        values = jax.random.randint(key_count, (homes // 2,), 0, TH + 1)
        values = values.at[0].set(TH)
        paired = jnp.stack([values, TH - values], axis=1).reshape(homes)
        counts = jnp.zeros((homes,), jnp.int32).at[order].set(paired.astype(jnp.int32))
        scores = jax.random.randint(key_pick, (homes, TH), 0, 1 << 20) * TH + jnp.arange(TH)[None, :]
        placed = jnp.argsort(jnp.argsort(scores, axis=1), axis=1)
        live = (placed < counts[:, None]).reshape(homes * TH).astype(jnp.int32)
        ranking = jnp.cumsum(live) - 1
        return jnp.where(live > 0, ranking % homes, -1).astype(jnp.int32)
    return jax.vmap(one_year)(jax.random.split(key, YEARS))


def levels(key, dims, pieces, least, high):
    factor_of, own = 1.0, jax.random.fold_in(key, 6)
    for position, parts in pieces:
        draws = jnp.exp(jax.random.uniform(jax.random.fold_in(own, position), (parts,), jnp.float32, least / len(pieces), high / len(pieces)))
        factor_of = factor_of * jnp.repeat(draws, dims[position] // parts).reshape([-1 if axis == position else 1 for axis in range(len(dims))])
    return factor_of


def normal_values(own_key, shape, width, reach, cuts=(), held_as=jnp.bfloat16):
    drawn = width * jax.random.normal(own_key, shape, jnp.float32)
    if cuts:
        drawn = drawn * levels(own_key, shape, cuts, -0.22, 0.18)
    return jnp.clip(drawn, -reach, reach).astype(held_as)


def setup_inputs(seed: int = 0) -> dict:
    splits = jax.random.split(jax.random.key(seed), 8)
    return {
        "forcing": normal_values(splits[0], (YEARS, TILES, CIN, TILE_ROWS, TILE_COLS), 1.0, 6.0, ((0, 4), (1, 8))),
        "hidden_prev": jnp.clip(jax.random.uniform(splits[1], (YEARS, TILES, HID, TILE_ROWS, TILE_COLS), jnp.float32, -0.8984375, 0.8984375) * levels(splits[1], (YEARS, TILES, HID, TILE_ROWS, TILE_COLS), ((0, 4), (1, 8)), -0.4, 0.0), -0.8984375, 0.8984375).astype(jnp.bfloat16),
        "cell_prev": normal_values(splits[2], (YEARS, TILES, HID, TILE_ROWS, TILE_COLS), 1.0, 4.0, ((0, 4), (1, 8))),
        "hidden_grad": normal_values(splits[3], (YEARS, TILES, HID, TILE_ROWS, TILE_COLS), (3.0 / (YEARS * TILES * TILE_ROWS * TILE_COLS) ** 0.5), 0.0625, ((0, 4), (1, 8))),
        "w_gates": normal_values(splits[4], (GATES, 9 * KIN), (9 * KIN) ** -0.5, 0.21875),
        "gate_bias": normal_values(splits[5], (GATES,), 1.0, 4.0, (), jnp.float32),
        "worker": draw_worker(jax.random.fold_in(splits[7], 71), 0),
    }


def tile_step(window, cell_old, out_grad, flag, w_gates, gate_bias):
    in_width, rows_pad, cols_pad = window.shape
    tile_rows = rows_pad - 2
    tile_cols = cols_pad - 2
    hidden_width = cell_old.shape[0]
    cells = tile_rows * tile_cols
    patches = jnp.concatenate([window[:, row_off:row_off + tile_rows, col_off:col_off + tile_cols].reshape(in_width, cells) for row_off in range(3) for col_off in range(3)], axis=0)
    pre = jnp.dot(w_gates, patches, preferred_element_type=jnp.float32) + gate_bias[:, None]
    pre = pre.reshape(4, hidden_width, cells)
    in_gate = jax.nn.sigmoid(pre[0])
    forget_gate = jax.nn.sigmoid(pre[1])
    out_gate = jax.nn.sigmoid(pre[2])
    candidate = jnp.tanh(pre[3])
    cell_before = cell_old.reshape(hidden_width, cells).astype(jnp.float32)
    cell_full = forget_gate * cell_before + in_gate * candidate
    squashed = jnp.tanh(cell_full)
    hidden_full = out_gate * squashed
    upstream = out_grad.reshape(hidden_width, cells).astype(jnp.float32)
    d_cell = upstream * out_gate * (1.0 - squashed * squashed)
    gate_grad = jnp.concatenate([
        d_cell * candidate * in_gate * (1.0 - in_gate),
        d_cell * cell_before * forget_gate * (1.0 - forget_gate),
        upstream * squashed * out_gate * (1.0 - out_gate),
        d_cell * in_gate * (1.0 - candidate * candidate)], axis=0)
    gate_grad = (gate_grad * flag).astype(jnp.bfloat16)
    weight_part = lax.dot_general(gate_grad, patches, (((1,), (1,)), ((), ())), preferred_element_type=jnp.float32)
    bias_part = jnp.sum(gate_grad.astype(jnp.float32), axis=1)
    hidden_new = hidden_full.astype(jnp.bfloat16).reshape(hidden_width, tile_rows, tile_cols)
    cell_new = cell_full.astype(jnp.bfloat16).reshape(hidden_width, tile_rows, tile_cols)
    return hidden_new, cell_new, weight_part, bias_part


def reference(forcing, hidden_prev, cell_prev, hidden_grad, w_gates, gate_bias, worker):
    years, tiles, in_ch, tile_rows, tile_cols = forcing.shape
    in_width = in_ch + hidden_prev.shape[2]
    homes = tiles // TH
    active_count = homes * CAP
    grad_weights = jnp.zeros(w_gates.shape, jnp.float32)
    grad_bias = jnp.zeros(gate_bias.shape, jnp.float32)
    hidden_list = []
    cell_list = []
    for year in range(years):
        joined = jnp.concatenate([forcing[year], hidden_prev[year]], axis=1)
        framed = joined.reshape(tiles // TW, TW, in_width, tile_rows, tile_cols).transpose(2, 0, 3, 1, 4)
        framed = framed.reshape(in_width, (tiles // TW) * tile_rows, TW * tile_cols)
        framed = jnp.pad(framed, ((0, 0), (1, 1), (1, 1)))
        live = worker[year] >= 0
        chosen = jnp.nonzero(live, size=active_count)[0].astype(jnp.int32)
        cell_year = cell_prev[year]
        grad_year = hidden_grad[year]

        def one_tile(carry, tile_id):
            row_start = (tile_id // TW) * tile_rows
            col_start = (tile_id % TW) * tile_cols
            window = lax.dynamic_slice(framed, (jnp.int32(0), row_start.astype(jnp.int32), col_start.astype(jnp.int32)), (in_width, tile_rows + 2, tile_cols + 2))
            hidden_new, cell_new, weight_part, bias_part = tile_step(window, cell_year[tile_id], grad_year[tile_id], jnp.float32(1.0), w_gates, gate_bias)
            return (carry[0] + weight_part, carry[1] + bias_part), (hidden_new, cell_new)

        (grad_weights, grad_bias), (hidden_done, cell_done) = lax.scan(one_tile, (grad_weights, grad_bias), chosen)
        hidden_list.append(hidden_prev[year].at[chosen].set(hidden_done))
        cell_list.append(cell_prev[year].at[chosen].set(cell_done))
    return jnp.stack(hidden_list), jnp.stack(cell_list), grad_weights, grad_bias
```

```python
import functools

import jax
import jax.numpy as jnp
from jax import lax
from jax.experimental import pallas as pl
from jax.experimental.pallas import tpu as pltpu
from jax.sharding import PartitionSpec as P

TW = 4
MESH = pl.DeviceIdType.MESH
CHUNK = 16


def halo_kernel(n, forcing, hidden, out, f_edge, h_edge, stage, send, landed, in_sem, send_sem, recv_sem):
    _, tiles, in_ch, rows, cols = forcing.shape
    width = in_ch + hidden.shape[2]
    me = lax.axis_index("space")
    loads = []
    for edge, first in ((0, 0), (1, tiles - TW)):
        loads.append(
            (
                pltpu.make_async_copy(
                    forcing.at[0, pl.ds(first, TW)], f_edge.at[edge], in_sem.at[2 * edge]
                ),
                pltpu.make_async_copy(
                    hidden.at[0, pl.ds(first, TW)], h_edge.at[edge], in_sem.at[2 * edge + 1]
                ),
            )
        )
    for pair in loads:
        for copy in pair:
            copy.start()
    barrier = pltpu.get_barrier_semaphore()
    has_up, has_down = me > 0, me < n - 1

    @pl.when(has_up)
    def _():
        pl.semaphore_signal(barrier, inc=1, device_id={"space": me - 1}, device_id_type=MESH)

    @pl.when(has_down)
    def _():
        pl.semaphore_signal(barrier, inc=1, device_id={"space": me + 1}, device_id_type=MESH)

    for edge, row in ((0, 0), (1, rows - 1)):
        for copy in loads[edge]:
            copy.wait()
        for tile in range(TW):
            stage[0 : in_ch * rows] = f_edge[edge, tile].astype(jnp.float32).reshape(in_ch * rows, cols)
            stage[in_ch * rows :] = (
                h_edge[edge, tile].astype(jnp.float32).reshape((width - in_ch) * rows, cols)
            )
            line = stage[pl.ds(row, width, stride=rows), :]
            send[edge, :, tile * cols : (tile + 1) * cols] = line.astype(jnp.bfloat16)

    pl.semaphore_wait(barrier, jnp.where(has_up, 1, 0) + jnp.where(has_down, 1, 0))

    def to_up():
        return pltpu.make_async_remote_copy(
            src_ref=send.at[0], dst_ref=landed.at[1], send_sem=send_sem.at[0],
            recv_sem=recv_sem.at[1], device_id={"space": me - 1}, device_id_type=MESH,
        )

    def to_down():
        return pltpu.make_async_remote_copy(
            src_ref=send.at[1], dst_ref=landed.at[0], send_sem=send_sem.at[1],
            recv_sem=recv_sem.at[0], device_id={"space": me + 1}, device_id_type=MESH,
        )

    @pl.when(has_up)
    def _():
        to_up().start()

    @pl.when(has_down)
    def _():
        to_down().start()

    @pl.when(has_up)
    def _():
        to_up().wait_send()
        to_down().wait_recv()
        out[0] = landed[0]

    @pl.when(jnp.logical_not(has_up))
    def _():
        out[0] = jnp.zeros(out.shape[1:], out.dtype)

    @pl.when(has_down)
    def _():
        to_down().wait_send()
        to_up().wait_recv()
        out[1] = landed[1]

    @pl.when(jnp.logical_not(has_down))
    def _():
        out[1] = jnp.zeros(out.shape[1:], out.dtype)


def exchange_halo(forcing, hidden, n):
    _, tiles, in_ch, rows, cols = forcing.shape
    hid = hidden.shape[2]
    width = in_ch + hid
    edge = (2, width, TW * cols)
    return pl.pallas_call(
        functools.partial(halo_kernel, n),
        out_shape=jax.ShapeDtypeStruct(edge, jnp.bfloat16),
        in_specs=[pl.BlockSpec(memory_space=pl.ANY)] * 2,
        out_specs=pl.BlockSpec(memory_space=pltpu.VMEM),
        scratch_shapes=[
            pltpu.VMEM((2, TW, in_ch, rows, cols), jnp.bfloat16),
            pltpu.VMEM((2, TW, hid, rows, cols), jnp.bfloat16),
            pltpu.VMEM((width * rows, cols), jnp.float32),
            pltpu.VMEM(edge, jnp.bfloat16),
            pltpu.VMEM(edge, jnp.bfloat16),
            pltpu.SemaphoreType.DMA((4,)),
            pltpu.SemaphoreType.DMA((2,)),
            pltpu.SemaphoreType.DMA((2,)),
        ],
        compiler_params=pltpu.CompilerParams(collective_id=0, has_side_effects=True),
        name="halo",
    )(forcing, hidden)


def step_kernel(
    flags, halo, forcing, hidden, cell, grad, w_gates, gate_bias,
    hidden_out, cell_out, acc_out,
    fv, hv, cv, gv, ho, co, field, stage, cs, gs, hs, ns, wbuf, bbuf, pre, gate, bias_acc,
    f_sem, h_sem, c_sem, g_sem, ho_sem, co_sem,
):
    _, tiles, in_ch, rows, cols = forcing.shape
    hid = hidden.shape[2]
    width = in_ch + hid
    bands = tiles // TW
    span = TW * cols
    gates, depth = w_gates.shape
    padded = wbuf.shape[1]
    per = 3 * width

    def load(src, dst, sem, i):
        return pltpu.make_async_copy(
            src.at[0, pl.ds(i * TW, TW)], dst.at[pl.ds(i * TW, TW)], sem.at[i]
        )

    def store(src, dst, sem, i):
        return pltpu.make_async_copy(
            src.at[pl.ds(i * TW, TW)], dst.at[0, pl.ds(i * TW, TW)], sem.at[i]
        )

    for i in range(bands):
        load(forcing, fv, f_sem, i).start()
        load(hidden, hv, h_sem, i).start()
    for i in range(bands):
        load(cell, cv, c_sem, i).start()
        load(grad, gv, g_sem, i).start()

    row = lax.broadcasted_iota(jnp.int32, (gates, 1), 0)
    half = jnp.where(row < 3 * hid, 0.5, 1.0).astype(jnp.float32)
    wbuf[...] = jnp.zeros(wbuf.shape, wbuf.dtype)
    wbuf[:, 0:depth] = (w_gates[...].astype(jnp.float32) * half).astype(wbuf.dtype)
    bbuf[...] = jnp.broadcast_to(gate_bias[...] * half, bbuf.shape)
    acc_out[...] = jnp.zeros(acc_out.shape, acc_out.dtype)
    bias_acc[...] = jnp.zeros(bias_acc.shape, bias_acc.dtype)
    field[(bands * rows + 2) * per :, :] = jnp.zeros((padded - depth, span), field.dtype)

    lane = lax.broadcasted_iota(jnp.int32, (width, span), 1)

    def put_row(line, x):
        base = pl.multiple_of(line * per, 16)
        left = jnp.where(lane == 0, 0.0, pltpu.roll(x, 1, 1))
        right = jnp.where(lane == span - 1, 0.0, pltpu.roll(x, span - 1, 1))
        field[pl.ds(base, width), :] = left.astype(field.dtype)
        field[pl.ds(pl.multiple_of(base + width, 16), width), :] = x.astype(field.dtype)
        field[pl.ds(pl.multiple_of(base + 2 * width, 16), width), :] = right.astype(field.dtype)

    put_row(0, halo[0].astype(jnp.float32))
    put_row(bands * rows + 1, halo[1].astype(jnp.float32))

    @pl.loop(0, bands)
    def _(i):
        load(forcing, fv, f_sem, i).wait()
        load(hidden, hv, h_sem, i).wait()
        for tile in range(TW):
            base = tile * width * rows
            stage[base : base + in_ch * rows] = (
                fv[i * TW + tile].astype(jnp.float32).reshape(in_ch * rows, cols)
            )
            stage[base + in_ch * rows : base + width * rows] = (
                hv[i * TW + tile].astype(jnp.float32).reshape(hid * rows, cols)
            )
        for r in range(rows):
            x = jnp.concatenate(
                [stage[pl.ds(tile * width * rows + r, width, stride=rows), :] for tile in range(TW)],
                axis=1,
            )
            put_row(i * rows + r + 1, x)

    @pl.loop(0, bands)
    def _(i):
        load(cell, cv, c_sem, i).wait()
        load(grad, gv, g_sem, i).wait()
        for tile in range(TW):
            live = jnp.where(flags[i * TW + tile] >= 0, 1.0, 0.0).astype(jnp.float32)
            lines = pl.ds(tile * hid * rows, hid * rows)
            cs[lines] = cv[i * TW + tile].astype(jnp.float32).reshape(hid * rows, cols)
            gs[lines] = gv[i * TW + tile].astype(jnp.float32).reshape(hid * rows, cols) * live
        for r in range(rows):
            start = pl.multiple_of((i * rows + r) * per, 16)
            slot = r % 2
            patches = field[pl.ds(start, padded), :]
            pre[slot] = jnp.dot(wbuf[...], patches, preferred_element_type=jnp.float32)
            for ch in range(0, hid, CHUNK):
                for tile in range(TW):
                    at = pl.ds(tile * hid * rows + ch * rows + r, CHUNK, stride=rows)
                    c0, c1 = tile * cols, (tile + 1) * cols
                    parts = [
                        jnp.tanh(
                            pre[slot, g * hid + ch : g * hid + ch + CHUNK, c0:c1]
                            + bbuf[g * hid + ch : g * hid + ch + CHUNK, :]
                        )
                        for g in range(4)
                    ]
                    t_in, t_forget, t_out, cand = parts
                    in_gate = 0.5 * t_in + 0.5
                    forget = 0.5 * t_forget + 0.5
                    out_gate = 0.5 * t_out + 0.5
                    before = cs[at, :]
                    up = gs[at, :]
                    now = forget * before + in_gate * cand
                    squashed = jnp.tanh(now)
                    hs[at, :] = out_gate * squashed
                    ns[at, :] = now
                    d_cell = up * out_gate * (1.0 - squashed * squashed)
                    grads = (
                        d_cell * cand * (1.0 - t_in * t_in),
                        d_cell * before * (1.0 - t_forget * t_forget),
                        up * squashed * (1.0 - t_out * t_out),
                        d_cell * in_gate * (1.0 - cand * cand),
                    )
                    for g in range(4):
                        lines = slice(g * hid + ch, g * hid + ch + CHUNK)
                        gate[slot, lines, c0:c1] = grads[g].astype(gate.dtype)
                        bias_acc[lines, :] += grads[g]
            acc_out[...] += lax.dot_general(
                gate[slot], patches, (((1,), (1,)), ((), ())), preferred_element_type=jnp.float32
            )
        for tile in range(TW):
            live = flags[i * TW + tile] >= 0
            lines = pl.ds(tile * hid * rows, hid * rows)
            where = i * TW + tile
            keep = jnp.where(live, 1.0, 0.0).astype(jnp.float32)
            alive = jnp.full((hid, rows, cols), keep) > 0.5
            ho[where] = jnp.where(
                alive, hs[lines].reshape(hid, rows, cols), hv[where].astype(jnp.float32)
            ).astype(ho.dtype)
            co[where] = jnp.where(
                alive, ns[lines].reshape(hid, rows, cols), cv[where].astype(jnp.float32)
            ).astype(co.dtype)
        store(ho, hidden_out, ho_sem, i).start()
        store(co, cell_out, co_sem, i).start()

    quarter = jnp.where(row < 3 * hid, 0.25, 1.0).astype(jnp.float32)
    bias_sum = jnp.sum(bias_acc[...], axis=1, keepdims=True) * quarter
    column = lax.broadcasted_iota(jnp.int32, (gates, padded), 1)
    acc_out[...] = jnp.where(
        column < depth, acc_out[...] * quarter, jnp.where(column == depth, bias_sum, 0.0)
    )
    for i in range(bands):
        store(ho, hidden_out, ho_sem, i).wait()
        store(co, cell_out, co_sem, i).wait()


def run_step(flags, halo, forcing, hidden, cell, grad, w_gates, gate_bias):
    _, tiles, in_ch, rows, cols = forcing.shape
    hid = hidden.shape[2]
    width = in_ch + hid
    bands = tiles // TW
    span = TW * cols
    gates, depth = w_gates.shape
    padded = -(-(depth + 1) // 256) * 256
    state = (tiles, hid, rows, cols)
    flat = (TW * hid * rows, cols)
    whole = pl.BlockSpec(memory_space=pl.ANY)
    vmem = pl.BlockSpec(memory_space=pltpu.VMEM)
    return pl.pallas_call(
        step_kernel,
        out_shape=(
            jax.ShapeDtypeStruct(hidden.shape, hidden.dtype),
            jax.ShapeDtypeStruct(cell.shape, cell.dtype),
            jax.ShapeDtypeStruct((gates, padded), jnp.float32),
        ),
        in_specs=[pl.BlockSpec(memory_space=pltpu.SMEM), vmem, whole, whole, whole, whole, vmem, vmem],
        out_specs=(whole, whole, vmem),
        scratch_shapes=[
            pltpu.VMEM((tiles, in_ch, rows, cols), jnp.bfloat16),
            pltpu.VMEM(state, jnp.bfloat16),
            pltpu.VMEM(state, jnp.bfloat16),
            pltpu.VMEM(state, jnp.bfloat16),
            pltpu.VMEM(state, jnp.bfloat16),
            pltpu.VMEM(state, jnp.bfloat16),
            pltpu.VMEM(((bands * rows + 2) * 3 * width + padded - depth, span), jnp.bfloat16),
            pltpu.VMEM((TW * width * rows, cols), jnp.float32),
            pltpu.VMEM(flat, jnp.float32),
            pltpu.VMEM(flat, jnp.float32),
            pltpu.VMEM(flat, jnp.float32),
            pltpu.VMEM(flat, jnp.float32),
            pltpu.VMEM((gates, padded), jnp.bfloat16),
            pltpu.VMEM((gates, cols), jnp.float32),
            pltpu.VMEM((2, gates, span), jnp.float32),
            pltpu.VMEM((2, gates, span), jnp.bfloat16),
            pltpu.VMEM((gates, cols), jnp.float32),
        ]
        + [pltpu.SemaphoreType.DMA((bands,))] * 6,
        compiler_params=pltpu.CompilerParams(vmem_limit_bytes=48 * 1024 * 1024),
        cost_estimate=pl.CostEstimate(
            flops=4 * gates * depth * tiles * rows * cols,
            bytes_accessed=12 * tiles * hid * rows * cols,
            transcendentals=5 * tiles * hid * rows * cols,
        ),
        name="step",
    )(flags, halo, forcing, hidden, cell, grad, w_gates, gate_bias)


def reduce_kernel(n_space, n_dp, acc, out, mine, first, second, part, third, s1, r1, s2, r2, s3, r3):
    sub = out.shape[0] // n_dp
    wide = acc.shape[1] // 2
    home, year = lax.axis_index("space"), lax.axis_index("dp")

    def years_off(off):
        return lax.rem(year + off, n_dp)

    def homes_off(off):
        return lax.rem(home + off, n_space)

    barrier = pltpu.get_barrier_semaphore()
    for off in range(1, n_dp):
        pl.semaphore_signal(barrier, inc=1, device_id={"dp": years_off(off)}, device_id_type=MESH)
    for off in range(1, n_space):
        pl.semaphore_signal(barrier, inc=1, device_id={"space": homes_off(off)}, device_id_type=MESH)

    for d in range(n_dp):
        for s in range(n_space):
            top = (s * n_dp + d) * sub
            mine[d, s] = jnp.concatenate(
                [acc[top : top + sub, 0:wide], acc[top : top + sub, wide:]], axis=0
            ).astype(mine.dtype)

    pl.semaphore_wait(barrier, n_dp + n_space - 2)

    copies = []
    for off in range(1, n_dp):
        copies.append(
            pltpu.make_async_remote_copy(
                src_ref=mine.at[years_off(off)], dst_ref=first.at[off - 1], send_sem=s1.at[off - 1],
                recv_sem=r1.at[off - 1], device_id={"dp": years_off(off)}, device_id_type=MESH,
            )
        )
        copies[-1].start()
    for copy in copies:
        copy.wait()
    total = mine[year].astype(jnp.float32)
    for off in range(1, n_dp):
        total = total + first[off - 1].astype(jnp.float32)
    part[...] = total.astype(part.dtype)

    copies = []
    for off in range(1, n_space):
        copies.append(
            pltpu.make_async_remote_copy(
                src_ref=part.at[homes_off(off)], dst_ref=second.at[off - 1], send_sem=s2.at[off - 1],
                recv_sem=r2.at[off - 1], device_id={"space": homes_off(off)}, device_id_type=MESH,
            )
        )
        copies[-1].start()
    for copy in copies:
        copy.wait()
    total = part[home].astype(jnp.float32)
    for off in range(1, n_space):
        total = total + second[off - 1].astype(jnp.float32)
    third[0] = total

    copies = []
    for off in range(1, n_dp):
        copies.append(
            pltpu.make_async_remote_copy(
                src_ref=third.at[0], dst_ref=third.at[off], send_sem=s3.at[off - 1],
                recv_sem=r3.at[off - 1], device_id={"dp": years_off(off)}, device_id_type=MESH,
            )
        )
        copies[-1].start()
    for copy in copies:
        copy.wait()
    for off in range(n_dp):
        whose = lax.rem(year - off + n_dp, n_dp)
        lines = pl.ds(pl.multiple_of(whose * sub, 8), sub)
        out[lines, 0:wide] = third[off, 0:sub, :]
        out[lines, wide:] = third[off, sub:, :]


def reduce_all(acc, n_space, n_dp):
    gates, padded = acc.shape
    keep = gates // n_space
    sub = keep // n_dp
    block = (2 * sub, padded // 2)
    vmem = pl.BlockSpec(memory_space=pltpu.VMEM)
    return pl.pallas_call(
        functools.partial(reduce_kernel, n_space, n_dp),
        out_shape=jax.ShapeDtypeStruct((keep, padded), jnp.float32),
        in_specs=[vmem],
        out_specs=vmem,
        scratch_shapes=[
            pltpu.VMEM((n_dp, n_space) + block, jnp.bfloat16),
            pltpu.VMEM((n_dp - 1, n_space) + block, jnp.bfloat16),
            pltpu.VMEM((n_space - 1,) + block, jnp.bfloat16),
            pltpu.VMEM((n_space,) + block, jnp.bfloat16),
            pltpu.VMEM((n_dp,) + block, jnp.float32),
            pltpu.SemaphoreType.DMA((n_dp - 1,)),
            pltpu.SemaphoreType.DMA((n_dp - 1,)),
            pltpu.SemaphoreType.DMA((n_space - 1,)),
            pltpu.SemaphoreType.DMA((n_space - 1,)),
            pltpu.SemaphoreType.DMA((n_dp - 1,)),
            pltpu.SemaphoreType.DMA((n_dp - 1,)),
        ],
        compiler_params=pltpu.CompilerParams(collective_id=1, has_side_effects=True),
        name="reduce",
    )(acc)


def shards(n_space, n_dp, forcing, hidden_prev, cell_prev, hidden_grad, w_gates, gate_bias, worker):
    tiles = forcing.shape[1]
    gates, depth = w_gates.shape
    mine = lax.dynamic_slice_in_dim(worker[0], lax.axis_index("space") * tiles, tiles)
    halo = exchange_halo(forcing, hidden_prev, n_space)
    hidden_next, cell_next, acc = run_step(
        mine, halo, forcing, hidden_prev, cell_prev, hidden_grad, w_gates, gate_bias[:, None]
    )
    if gates % (8 * n_space * n_dp) == 0:
        total = reduce_all(acc, n_space, n_dp)
    else:
        total = lax.psum_scatter(acc, "space", scatter_dimension=0, tiled=True)
        total = lax.psum(total, "dp")
    return hidden_next, cell_next, total[:, :depth], total[:, depth]


def solution(mesh):
    state = P("dp", "space", None, None, None)
    return jax.shard_map(
        functools.partial(shards, mesh.shape["space"], mesh.shape["dp"]),
        mesh=mesh,
        in_specs=(state, state, state, state, P(), P(), P("dp", None)),
        out_specs=(state, state, P("space", None), P("space")),
        check_vma=False,
    )
```

```python
import functools

import jax
import jax.numpy as jnp
from jax import lax
from jax.experimental import pallas as pl
from jax.experimental.pallas import tpu as pltpu
from jax.sharding import PartitionSpec as P

TW = 4
MESH = pl.DeviceIdType.MESH
CHUNK = 16
GROUP = 4


def halo_kernel(n, forcing, hidden, out, f_edge, h_edge, stage, send, landed, in_sem, send_sem, recv_sem):
    _, tiles, in_ch, rows, cols = forcing.shape
    width = in_ch + hidden.shape[2]
    me = lax.axis_index("space")
    loads = []
    for edge, first in ((0, 0), (1, tiles - TW)):
        loads.append(
            (
                pltpu.make_async_copy(
                    forcing.at[0, pl.ds(first, TW)], f_edge.at[edge], in_sem.at[2 * edge]
                ),
                pltpu.make_async_copy(
                    hidden.at[0, pl.ds(first, TW)], h_edge.at[edge], in_sem.at[2 * edge + 1]
                ),
            )
        )
    for pair in loads:
        for copy in pair:
            copy.start()
    barrier = pltpu.get_barrier_semaphore()
    has_up, has_down = me > 0, me < n - 1

    @pl.when(has_up)
    def _():
        pl.semaphore_signal(barrier, inc=1, device_id={"space": me - 1}, device_id_type=MESH)

    @pl.when(has_down)
    def _():
        pl.semaphore_signal(barrier, inc=1, device_id={"space": me + 1}, device_id_type=MESH)

    for edge, row in ((0, 0), (1, rows - 1)):
        for copy in loads[edge]:
            copy.wait()
        for tile in range(TW):
            stage[0 : in_ch * rows] = f_edge[edge, tile].astype(jnp.float32).reshape(in_ch * rows, cols)
            stage[in_ch * rows :] = (
                h_edge[edge, tile].astype(jnp.float32).reshape((width - in_ch) * rows, cols)
            )
            line = stage[pl.ds(row, width, stride=rows), :]
            send[edge, :, tile * cols : (tile + 1) * cols] = line.astype(jnp.bfloat16)

    pl.semaphore_wait(barrier, jnp.where(has_up, 1, 0) + jnp.where(has_down, 1, 0))

    def to_up():
        return pltpu.make_async_remote_copy(
            src_ref=send.at[0], dst_ref=landed.at[1], send_sem=send_sem.at[0],
            recv_sem=recv_sem.at[1], device_id={"space": me - 1}, device_id_type=MESH,
        )

    def to_down():
        return pltpu.make_async_remote_copy(
            src_ref=send.at[1], dst_ref=landed.at[0], send_sem=send_sem.at[1],
            recv_sem=recv_sem.at[0], device_id={"space": me + 1}, device_id_type=MESH,
        )

    @pl.when(has_up)
    def _():
        to_up().start()

    @pl.when(has_down)
    def _():
        to_down().start()

    @pl.when(has_up)
    def _():
        to_up().wait_send()
        to_down().wait_recv()
        out[0] = landed[0]

    @pl.when(jnp.logical_not(has_up))
    def _():
        out[0] = jnp.zeros(out.shape[1:], out.dtype)

    @pl.when(has_down)
    def _():
        to_down().wait_send()
        to_up().wait_recv()
        out[1] = landed[1]

    @pl.when(jnp.logical_not(has_down))
    def _():
        out[1] = jnp.zeros(out.shape[1:], out.dtype)


def exchange_halo(forcing, hidden, n):
    _, tiles, in_ch, rows, cols = forcing.shape
    hid = hidden.shape[2]
    width = in_ch + hid
    edge = (2, width, TW * cols)
    return pl.pallas_call(
        functools.partial(halo_kernel, n),
        out_shape=jax.ShapeDtypeStruct(edge, jnp.bfloat16),
        in_specs=[pl.BlockSpec(memory_space=pl.ANY)] * 2,
        out_specs=pl.BlockSpec(memory_space=pltpu.VMEM),
        scratch_shapes=[
            pltpu.VMEM((2, TW, in_ch, rows, cols), jnp.bfloat16),
            pltpu.VMEM((2, TW, hid, rows, cols), jnp.bfloat16),
            pltpu.VMEM((width * rows, cols), jnp.float32),
            pltpu.VMEM(edge, jnp.bfloat16),
            pltpu.VMEM(edge, jnp.bfloat16),
            pltpu.SemaphoreType.DMA((4,)),
            pltpu.SemaphoreType.DMA((2,)),
            pltpu.SemaphoreType.DMA((2,)),
        ],
        compiler_params=pltpu.CompilerParams(collective_id=0, has_side_effects=True),
        name="halo",
    )(forcing, hidden)


def step_kernel(
    flags, halo, forcing, hidden, cell, grad, w_gates, gate_bias,
    hidden_out, cell_out, sums_out,
    fv, hv, cv, gv, ho, co, field, stage, cs, gs, hs, ns, wbuf, bbuf, pre, gate, bias_acc,
    edges, wt, acc, sums, f_sem, h_sem, c_sem, g_sem, ho_sem, co_sem, x_sem,
):
    _, tiles, in_ch, rows, cols = forcing.shape
    hid = hidden.shape[2]
    width = in_ch + hid
    bands = tiles // TW
    span = TW * cols
    depth, gates = w_gates.shape
    padded = wbuf.shape[1]
    per = 3 * width
    get_edges = pltpu.make_async_copy(halo, edges, x_sem.at[0])
    get_weights = pltpu.make_async_copy(w_gates, wt.at[pl.ds(0, depth)], x_sem.at[1])
    put_sums = pltpu.make_async_copy(sums, sums_out, x_sem.at[2])

    def load(src, dst, sem, i):
        return pltpu.make_async_copy(
            src.at[0, pl.ds(i * TW, TW)], dst.at[pl.ds(i * TW, TW)], sem.at[i]
        )

    def store(src, dst, sem, i):
        return pltpu.make_async_copy(
            src.at[pl.ds(i * TW, TW)], dst.at[0, pl.ds(i * TW, TW)], sem.at[i]
        )

    for i in range(bands):
        load(forcing, fv, f_sem, i).start()
        load(hidden, hv, h_sem, i).start()
    get_weights.start()
    get_edges.start()
    for i in range(bands):
        load(cell, cv, c_sem, i).start()
        load(grad, gv, g_sem, i).start()

    row = lax.broadcasted_iota(jnp.int32, (gates, 1), 0)
    half = jnp.where(row < 3 * hid, 0.5, 1.0).astype(jnp.float32)
    wt[depth:, :] = jnp.zeros((padded - depth, gates), wt.dtype)
    bbuf[...] = jnp.broadcast_to(gate_bias[...], (cols, gates)).T * half
    acc[...] = jnp.zeros(acc.shape, acc.dtype)
    bias_acc[...] = jnp.zeros(bias_acc.shape, bias_acc.dtype)
    field[(bands * rows + 2) * per :, :] = jnp.zeros((padded - depth, span), field.dtype)

    lane = lax.broadcasted_iota(jnp.int32, (width, span), 1)

    def put_row(line, x):
        base = pl.multiple_of(line * per, 16)
        left = jnp.where(lane == 0, 0.0, pltpu.roll(x, 1, 1))
        right = jnp.where(lane == span - 1, 0.0, pltpu.roll(x, span - 1, 1))
        field[pl.ds(base, width), :] = left.astype(field.dtype)
        field[pl.ds(pl.multiple_of(base + width, 16), width), :] = x.astype(field.dtype)
        field[pl.ds(pl.multiple_of(base + 2 * width, 16), width), :] = right.astype(field.dtype)

    @pl.loop(0, bands)
    def _(i):
        load(forcing, fv, f_sem, i).wait()
        load(hidden, hv, h_sem, i).wait()
        for tile in range(TW):
            base = tile * width * rows
            stage[base : base + in_ch * rows] = (
                fv[i * TW + tile].astype(jnp.float32).reshape(in_ch * rows, cols)
            )
            stage[base + in_ch * rows : base + width * rows] = (
                hv[i * TW + tile].astype(jnp.float32).reshape(hid * rows, cols)
            )
        for r in range(rows):
            x = jnp.concatenate(
                [stage[pl.ds(tile * width * rows + r, width, stride=rows), :] for tile in range(TW)],
                axis=1,
            )
            put_row(i * rows + r + 1, x)

    get_weights.wait()
    wbuf[...] = (wt[...].astype(jnp.float32).T * half).astype(wbuf.dtype)
    get_edges.wait()
    put_row(0, edges[0].astype(jnp.float32))
    put_row(bands * rows + 1, edges[1].astype(jnp.float32))

    @pl.loop(0, bands)
    def _(i):
        load(cell, cv, c_sem, i).wait()
        load(grad, gv, g_sem, i).wait()

        def patches(r):
            return field[pl.ds(pl.multiple_of((i * rows + r) * per, 16), padded), :]

        def forward(r):
            pre[r % 2] = jnp.dot(wbuf[...], patches(r), preferred_element_type=jnp.float32)

        def backward(group):
            seen = jnp.concatenate([patches(r) for r in range(group * GROUP, (group + 1) * GROUP)], axis=1)
            acc[...] += lax.dot_general(
                seen, gate[group % 2], (((1,), (1,)), ((), ())), preferred_element_type=jnp.float32
            )

        def pointwise(r):
            slot, group = r % 2, r // GROUP
            for ch in range(0, hid, CHUNK):
                lines = [slice(g * hid + ch, g * hid + ch + CHUNK) for g in range(4)]
                bias = [bbuf[lines[g], :] for g in range(4)]
                totals = [None] * 4
                for tile in range(TW):
                    at = pl.ds(tile * hid * rows + ch * rows + r, CHUNK, stride=rows)
                    c0, c1 = tile * cols, (tile + 1) * cols
                    t_in, t_forget, t_out, cand = [
                        jnp.tanh(pre[slot, lines[g], c0:c1] + bias[g]) for g in range(4)
                    ]
                    in_gate = 0.5 * t_in + 0.5
                    forget = 0.5 * t_forget + 0.5
                    out_gate = 0.5 * t_out + 0.5
                    before = cs[at, :]
                    up = gs[at, :]
                    now = forget * before + in_gate * cand
                    squashed = jnp.tanh(now)
                    hs[at, :] = out_gate * squashed
                    ns[at, :] = now
                    d_cell = up * out_gate * (1.0 - squashed * squashed)
                    grads = (
                        d_cell * cand * (1.0 - t_in * t_in),
                        d_cell * before * (1.0 - t_forget * t_forget),
                        up * squashed * (1.0 - t_out * t_out),
                        d_cell * in_gate * (1.0 - cand * cand),
                    )
                    d0 = (r % GROUP) * span + c0
                    for g in range(4):
                        gate[group % 2, lines[g], d0 : d0 + cols] = grads[g].astype(gate.dtype)
                        totals[g] = grads[g] if totals[g] is None else totals[g] + grads[g]
                for g in range(4):
                    bias_acc[lines[g], :] += totals[g]

        forward(0)
        for tile in range(TW):
            live = jnp.where(flags[i * TW + tile] >= 0, 1.0, 0.0).astype(jnp.float32)
            lines = pl.ds(tile * hid * rows, hid * rows)
            cs[lines] = cv[i * TW + tile].astype(jnp.float32).reshape(hid * rows, cols)
            gs[lines] = gv[i * TW + tile].astype(jnp.float32).reshape(hid * rows, cols) * live
        for r in range(rows):
            if r + 1 < rows:
                forward(r + 1)
            if r % GROUP == 0 and r > 0:
                backward(r // GROUP - 1)
            pointwise(r)
        backward(rows // GROUP - 1)
        for tile in range(TW):
            live = flags[i * TW + tile] >= 0
            lines = pl.ds(tile * hid * rows, hid * rows)
            where = i * TW + tile
            keep = jnp.where(live, 1.0, 0.0).astype(jnp.float32)
            alive = jnp.full((hid, rows, cols), keep) > 0.5
            ho[where] = jnp.where(
                alive, hs[lines].reshape(hid, rows, cols), hv[where].astype(jnp.float32)
            ).astype(ho.dtype)
            co[where] = jnp.where(
                alive, ns[lines].reshape(hid, rows, cols), cv[where].astype(jnp.float32)
            ).astype(co.dtype)
        store(ho, hidden_out, ho_sem, i).start()
        store(co, cell_out, co_sem, i).start()

    quarter = jnp.where(row < 3 * hid, 0.25, 1.0).astype(jnp.float32)
    bias_sum = jnp.sum(bias_acc[...], axis=1, keepdims=True) * quarter
    column = lax.broadcasted_iota(jnp.int32, (gates, padded), 1)
    done = jnp.where(
        column < depth, acc[...].T * quarter, jnp.where(column == depth, bias_sum, 0.0)
    )
    if len(sums.shape) == 2:
        sums[...] = done
    else:
        n_dp, n_space = sums.shape[:2]
        sub, wide = gates // (n_dp * n_space), padded // 2
        for d in range(n_dp):
            for s in range(n_space):
                top = (s * n_dp + d) * sub
                sums[d, s] = jnp.concatenate(
                    [done[top : top + sub, 0:wide], done[top : top + sub, wide:]], axis=0
                ).astype(sums.dtype)
    put_sums.start()
    put_sums.wait()
    for i in range(bands):
        store(ho, hidden_out, ho_sem, i).wait()
        store(co, cell_out, co_sem, i).wait()


def run_step(sums, flags, halo, forcing, hidden, cell, grad, w_gates, gate_bias):
    _, tiles, in_ch, rows, cols = forcing.shape
    hid = hidden.shape[2]
    width = in_ch + hid
    bands = tiles // TW
    span = TW * cols
    depth, gates = w_gates.shape
    padded = -(-(depth + 1) // 256) * 256
    state = (tiles, hid, rows, cols)
    flat = (TW * hid * rows, cols)
    whole = pl.BlockSpec(memory_space=pl.ANY)
    vmem = pl.BlockSpec(memory_space=pltpu.VMEM)
    return pl.pallas_call(
        step_kernel,
        out_shape=(
            jax.ShapeDtypeStruct(hidden.shape, hidden.dtype),
            jax.ShapeDtypeStruct(cell.shape, cell.dtype),
            sums,
        ),
        in_specs=[pl.BlockSpec(memory_space=pltpu.SMEM), whole, whole, whole, whole, whole, whole, vmem],
        out_specs=(whole, whole, whole),
        scratch_shapes=[
            pltpu.VMEM((tiles, in_ch, rows, cols), jnp.bfloat16),
            pltpu.VMEM(state, jnp.bfloat16),
            pltpu.VMEM(state, jnp.bfloat16),
            pltpu.VMEM(state, jnp.bfloat16),
            pltpu.VMEM(state, jnp.bfloat16),
            pltpu.VMEM(state, jnp.bfloat16),
            pltpu.VMEM(((bands * rows + 2) * 3 * width + padded - depth, span), jnp.bfloat16),
            pltpu.VMEM((TW * width * rows, cols), jnp.float32),
            pltpu.VMEM(flat, jnp.float32),
            pltpu.VMEM(flat, jnp.float32),
            pltpu.VMEM(flat, jnp.float32),
            pltpu.VMEM(flat, jnp.float32),
            pltpu.VMEM((gates, padded), jnp.bfloat16),
            pltpu.VMEM((gates, cols), jnp.float32),
            pltpu.VMEM((2, gates, span), jnp.float32),
            pltpu.VMEM((2, gates, GROUP * span), jnp.bfloat16),
            pltpu.VMEM((gates, cols), jnp.float32),
            pltpu.VMEM(halo.shape, halo.dtype),
            pltpu.VMEM((padded, gates), jnp.bfloat16),
            pltpu.VMEM((padded, gates), jnp.float32),
            pltpu.VMEM(sums.shape, sums.dtype),
        ]
        + [pltpu.SemaphoreType.DMA((bands,))] * 6
        + [pltpu.SemaphoreType.DMA((3,))],
        compiler_params=pltpu.CompilerParams(vmem_limit_bytes=60 * 1024 * 1024),
        cost_estimate=pl.CostEstimate(
            flops=4 * gates * depth * tiles * rows * cols,
            bytes_accessed=12 * tiles * hid * rows * cols,
            transcendentals=5 * tiles * hid * rows * cols,
        ),
        name="step",
    )(flags, halo, forcing, hidden, cell, grad, w_gates, gate_bias)


def reduce_kernel(n_space, n_dp, sums, out, mine, first, second, part, third, own, s1, r1, s2, r2, s3, r3):
    sub = out.shape[0] // n_dp
    wide = sums.shape[-1]
    home, year = lax.axis_index("space"), lax.axis_index("dp")

    def years_off(off):
        return lax.rem(year + off, n_dp)

    def homes_off(off):
        return lax.rem(home + off, n_space)

    def over_years(off, place):
        return pltpu.make_async_remote_copy(
            src_ref=sums.at[years_off(off), homes_off(place)], dst_ref=first.at[off - 1, place],
            send_sem=s1.at[off - 1, place], recv_sem=r1.at[off - 1, place],
            device_id={"dp": years_off(off)}, device_id_type=MESH,
        )

    def over_homes(off):
        return pltpu.make_async_remote_copy(
            src_ref=part.at[off], dst_ref=second.at[off - 1], send_sem=s2.at[off - 1],
            recv_sem=r2.at[off - 1], device_id={"space": homes_off(off)}, device_id_type=MESH,
        )

    def to_years(off):
        return pltpu.make_async_remote_copy(
            src_ref=third.at[0], dst_ref=third.at[off], send_sem=s3.at[off - 1],
            recv_sem=r3.at[off - 1], device_id={"dp": years_off(off)}, device_id_type=MESH,
        )

    barrier = pltpu.get_barrier_semaphore()
    for off in range(1, n_dp):
        pl.semaphore_signal(barrier, inc=1, device_id={"dp": years_off(off)}, device_id_type=MESH)
    for off in range(1, n_space):
        pl.semaphore_signal(barrier, inc=1, device_id={"space": homes_off(off)}, device_id_type=MESH)
    get_mine = pltpu.make_async_copy(sums.at[year], mine, own)
    get_mine.start()
    pl.semaphore_wait(barrier, n_dp + n_space - 2)

    order = list(range(1, n_space)) + [0]
    for place in order:
        for off in range(1, n_dp):
            over_years(off, place).start()
    get_mine.wait()
    for place in order:
        total = mine[homes_off(place)].astype(jnp.float32)
        for off in range(1, n_dp):
            over_years(off, place).wait_recv()
            total = total + first[off - 1, place].astype(jnp.float32)
        if place:
            part[place] = total.astype(part.dtype)
            over_homes(place).start()
    for off in range(1, n_space):
        over_homes(off).wait_recv()
        total = total + second[off - 1].astype(jnp.float32)
    third[0] = total
    for off in range(1, n_dp):
        to_years(off).start()
    for off in range(n_dp):
        if off:
            to_years(off).wait_recv()
        whose = lax.rem(year - off + n_dp, n_dp)
        lines = pl.ds(pl.multiple_of(whose * sub, 8), sub)
        out[lines, 0:wide] = third[off, 0:sub, :]
        out[lines, wide:] = third[off, sub:, :]
    for place in order:
        for off in range(1, n_dp):
            over_years(off, place).wait_send()
    for off in range(1, n_space):
        over_homes(off).wait_send()
    for off in range(1, n_dp):
        to_years(off).wait_send()


def reduce_all(sums, gates):
    n_dp, n_space, _, wide = sums.shape
    keep = gates // n_space
    block = sums.shape[2:]
    return pl.pallas_call(
        functools.partial(reduce_kernel, n_space, n_dp),
        out_shape=jax.ShapeDtypeStruct((keep, 2 * wide), jnp.float32),
        in_specs=[pl.BlockSpec(memory_space=pl.ANY)],
        out_specs=pl.BlockSpec(memory_space=pltpu.VMEM),
        scratch_shapes=[
            pltpu.VMEM((n_space,) + block, jnp.bfloat16),
            pltpu.VMEM((n_dp - 1, n_space) + block, jnp.bfloat16),
            pltpu.VMEM((n_space - 1,) + block, jnp.bfloat16),
            pltpu.VMEM((n_space,) + block, jnp.bfloat16),
            pltpu.VMEM((n_dp,) + block, jnp.float32),
            pltpu.SemaphoreType.DMA,
            pltpu.SemaphoreType.DMA((n_dp - 1, n_space)),
            pltpu.SemaphoreType.DMA((n_dp - 1, n_space)),
            pltpu.SemaphoreType.DMA((n_space - 1,)),
            pltpu.SemaphoreType.DMA((n_space - 1,)),
            pltpu.SemaphoreType.DMA((n_dp - 1,)),
            pltpu.SemaphoreType.DMA((n_dp - 1,)),
        ],
        compiler_params=pltpu.CompilerParams(collective_id=1, has_side_effects=True),
        name="reduce",
    )(sums)


def shards(n_space, n_dp, forcing, hidden_prev, cell_prev, hidden_grad, w_gates, gate_bias, worker):
    tiles = forcing.shape[1]
    gates, depth = w_gates.shape
    mine = lax.dynamic_slice_in_dim(worker[0], lax.axis_index("space") * tiles, tiles)
    halo = exchange_halo(forcing, hidden_prev, n_space)
    padded = -(-(depth + 1) // 256) * 256
    sub, ragged = divmod(gates, n_space * n_dp)
    staged = ragged == 0 and sub % 8 == 0
    sums = jax.ShapeDtypeStruct((gates, padded), jnp.float32)
    if staged:
        sums = jax.ShapeDtypeStruct((n_dp, n_space, 2 * sub, padded // 2), jnp.bfloat16)
    hidden_next, cell_next, sums = run_step(
        sums, mine, halo, forcing, hidden_prev, cell_prev, hidden_grad, w_gates.T, gate_bias[None, :]
    )
    if staged:
        total = reduce_all(sums, gates)
    else:
        total = lax.psum(lax.psum_scatter(sums, "space", scatter_dimension=0, tiled=True), "dp")
    return hidden_next, cell_next, total[:, :depth], total[:, depth]


def solution(mesh):
    state = P("dp", "space", None, None, None)
    return jax.shard_map(
        functools.partial(shards, mesh.shape["space"], mesh.shape["dp"]),
        mesh=mesh,
        in_specs=(state, state, state, state, P(), P(), P("dp", None)),
        out_specs=(state, state, P("space", None), P("space")),
        check_vma=False,
    )
```

```python
import functools

import jax
import jax.numpy as jnp
from jax import lax
from jax.experimental import pallas as pl
from jax.experimental.pallas import tpu as pltpu
from jax.sharding import PartitionSpec as P

TW = 4
MESH = pl.DeviceIdType.MESH
CHUNK = 16
GROUP = 2


def halo_kernel(n, forcing, hidden, out, f_edge, h_edge, stage, send, landed, in_sem, send_sem, recv_sem):
    _, tiles, in_ch, rows, cols = forcing.shape
    width = in_ch + hidden.shape[2]
    me = lax.axis_index("space")
    loads = []
    for edge, first in ((0, 0), (1, tiles - TW)):
        loads.append(
            (
                pltpu.make_async_copy(
                    forcing.at[0, pl.ds(first, TW)], f_edge.at[edge], in_sem.at[2 * edge]
                ),
                pltpu.make_async_copy(
                    hidden.at[0, pl.ds(first, TW)], h_edge.at[edge], in_sem.at[2 * edge + 1]
                ),
            )
        )
    for pair in loads:
        for copy in pair:
            copy.start()
    barrier = pltpu.get_barrier_semaphore()
    has_up, has_down = me > 0, me < n - 1

    @pl.when(has_up)
    def _():
        pl.semaphore_signal(barrier, inc=1, device_id={"space": me - 1}, device_id_type=MESH)

    @pl.when(has_down)
    def _():
        pl.semaphore_signal(barrier, inc=1, device_id={"space": me + 1}, device_id_type=MESH)

    for edge, row in ((0, 0), (1, rows - 1)):
        for copy in loads[edge]:
            copy.wait()
        for tile in range(TW):
            stage[0 : in_ch * rows] = f_edge[edge, tile].astype(jnp.float32).reshape(in_ch * rows, cols)
            stage[in_ch * rows :] = (
                h_edge[edge, tile].astype(jnp.float32).reshape((width - in_ch) * rows, cols)
            )
            line = stage[pl.ds(row, width, stride=rows), :]
            send[edge, :, tile * cols : (tile + 1) * cols] = line.astype(jnp.bfloat16)

    pl.semaphore_wait(barrier, jnp.where(has_up, 1, 0) + jnp.where(has_down, 1, 0))

    def to_up():
        return pltpu.make_async_remote_copy(
            src_ref=send.at[0], dst_ref=landed.at[1], send_sem=send_sem.at[0],
            recv_sem=recv_sem.at[1], device_id={"space": me - 1}, device_id_type=MESH,
        )

    def to_down():
        return pltpu.make_async_remote_copy(
            src_ref=send.at[1], dst_ref=landed.at[0], send_sem=send_sem.at[1],
            recv_sem=recv_sem.at[0], device_id={"space": me + 1}, device_id_type=MESH,
        )

    @pl.when(has_up)
    def _():
        to_up().start()

    @pl.when(has_down)
    def _():
        to_down().start()

    @pl.when(has_up)
    def _():
        to_up().wait_send()
        to_down().wait_recv()
        out[0] = landed[0]

    @pl.when(jnp.logical_not(has_up))
    def _():
        out[0] = jnp.zeros(out.shape[1:], out.dtype)

    @pl.when(has_down)
    def _():
        to_down().wait_send()
        to_up().wait_recv()
        out[1] = landed[1]

    @pl.when(jnp.logical_not(has_down))
    def _():
        out[1] = jnp.zeros(out.shape[1:], out.dtype)


def exchange_halo(forcing, hidden, n):
    _, tiles, in_ch, rows, cols = forcing.shape
    hid = hidden.shape[2]
    width = in_ch + hid
    edge = (2, width, TW * cols)
    return pl.pallas_call(
        functools.partial(halo_kernel, n),
        out_shape=jax.ShapeDtypeStruct(edge, jnp.bfloat16),
        in_specs=[pl.BlockSpec(memory_space=pl.ANY)] * 2,
        out_specs=pl.BlockSpec(memory_space=pltpu.VMEM),
        scratch_shapes=[
            pltpu.VMEM((2, TW, in_ch, rows, cols), jnp.bfloat16),
            pltpu.VMEM((2, TW, hid, rows, cols), jnp.bfloat16),
            pltpu.VMEM((width * rows, cols), jnp.float32),
            pltpu.VMEM(edge, jnp.bfloat16),
            pltpu.VMEM(edge, jnp.bfloat16),
            pltpu.SemaphoreType.DMA((4,)),
            pltpu.SemaphoreType.DMA((2,)),
            pltpu.SemaphoreType.DMA((2,)),
        ],
        compiler_params=pltpu.CompilerParams(collective_id=0, has_side_effects=True),
        name="halo",
    )(forcing, hidden)


def step_kernel(
    flags, halo, forcing, hidden, cell, grad, w_gates, gate_bias,
    hidden_out, cell_out, sums_out,
    fv, hv, cv, gv, ho, co, field, stage, cs, gs, hs, ns, wbuf, bbuf, pre, gate, bias_acc,
    edges, wt, acc, sums, f_sem, h_sem, c_sem, g_sem, ho_sem, co_sem, x_sem,
):
    _, tiles, in_ch, rows, cols = forcing.shape
    hid = hidden.shape[2]
    width = in_ch + hid
    bands = tiles // TW
    span = TW * cols
    depth, gates = w_gates.shape
    padded = wbuf.shape[1]
    per = 3 * width
    get_edges = pltpu.make_async_copy(halo, edges, x_sem.at[0])
    get_weights = pltpu.make_async_copy(w_gates, wt.at[pl.ds(0, depth)], x_sem.at[1])
    put_sums = pltpu.make_async_copy(sums, sums_out, x_sem.at[2])

    def load(src, dst, sem, i):
        return pltpu.make_async_copy(
            src.at[0, pl.ds(i * TW, TW)], dst.at[pl.ds(i * TW, TW)], sem.at[i]
        )

    def store(src, dst, sem, i):
        return pltpu.make_async_copy(
            src.at[pl.ds(i * TW, TW)], dst.at[0, pl.ds(i * TW, TW)], sem.at[i]
        )

    for i in range(bands):
        load(forcing, fv, f_sem, i).start()
        load(hidden, hv, h_sem, i).start()
    get_weights.start()
    get_edges.start()
    for i in range(bands):
        load(cell, cv, c_sem, i).start()
        load(grad, gv, g_sem, i).start()

    row = lax.broadcasted_iota(jnp.int32, (gates, 1), 0)
    half = jnp.where(row < 3 * hid, 0.5, 1.0).astype(jnp.float32)
    wt[depth:, :] = jnp.zeros((padded - depth, gates), wt.dtype)
    bbuf[...] = jnp.broadcast_to(gate_bias[...], (cols, gates)).T * half
    acc[...] = jnp.zeros(acc.shape, acc.dtype)
    bias_acc[...] = jnp.zeros(bias_acc.shape, bias_acc.dtype)
    field[(bands * rows + 2) * per :, :] = jnp.zeros((per + padded - depth, span), field.dtype)

    lane = lax.broadcasted_iota(jnp.int32, (width, span), 1)

    def put_row(line, x):
        base = pl.multiple_of(line * per, 16)
        left = jnp.where(lane == 0, 0.0, pltpu.roll(x, 1, 1))
        right = jnp.where(lane == span - 1, 0.0, pltpu.roll(x, span - 1, 1))
        field[pl.ds(base, width), :] = left.astype(field.dtype)
        field[pl.ds(pl.multiple_of(base + width, 16), width), :] = x.astype(field.dtype)
        field[pl.ds(pl.multiple_of(base + 2 * width, 16), width), :] = right.astype(field.dtype)

    @pl.loop(0, bands)
    def _(i):
        load(forcing, fv, f_sem, i).wait()
        load(hidden, hv, h_sem, i).wait()
        for tile in range(TW):
            base = tile * width * rows
            stage[base : base + in_ch * rows] = (
                fv[i * TW + tile].astype(jnp.float32).reshape(in_ch * rows, cols)
            )
            stage[base + in_ch * rows : base + width * rows] = (
                hv[i * TW + tile].astype(jnp.float32).reshape(hid * rows, cols)
            )
        for r in range(rows):
            x = jnp.concatenate(
                [stage[pl.ds(tile * width * rows + r, width, stride=rows), :] for tile in range(TW)],
                axis=1,
            )
            put_row(i * rows + r + 1, x)

    get_weights.wait()
    wbuf[...] = (wt[...].astype(jnp.float32).T * half).astype(wbuf.dtype)
    get_edges.wait()
    put_row(0, edges[0].astype(jnp.float32))
    put_row(bands * rows + 1, edges[1].astype(jnp.float32))

    base_tile = lax.axis_index("space") * tiles
    gate[...] = jnp.zeros(gate.shape, gate.dtype)

    def patches(line, c0=0, c1=span):
        return field[pl.ds(pl.multiple_of(line * per, 16), padded), c0:c1]

    def forward(line, slot, part):
        c0, c1 = part * (span // 2), (part + 1) * (span // 2)
        pre[slot, :, c0:c1] = jnp.dot(
            wbuf[...], patches(line, c0, c1), preferred_element_type=jnp.float32
        )

    def backward(line, slot, part):
        lines = slice(part * (padded // 2), (part + 1) * (padded // 2))
        seen = jnp.concatenate(
            [
                field[pl.ds(pl.multiple_of((line + k) * per + lines.start, 16), padded // 2), :]
                for k in range(GROUP)
            ],
            axis=1,
        )
        acc[lines, :] += lax.dot_general(
            seen, gate[slot], (((1,), (1,)), ((), ())), preferred_element_type=jnp.float32
        )

    def stage_state(band, into, tile, c0, c1):
        slot = lax.rem(into, 2)
        live = jnp.where(flags[0, base_tile + band * TW + tile] >= 0, 1.0, 0.0).astype(jnp.float32)
        lines = pl.ds((tile * hid + c0) * rows, (c1 - c0) * rows)
        flat = ((c1 - c0) * rows, cols)
        cs[slot, lines] = cv[band * TW + tile, c0:c1].astype(jnp.float32).reshape(flat)
        gs[slot, lines] = gv[band * TW + tile, c0:c1].astype(jnp.float32).reshape(flat) * live

    def pointwise(i, r, between):
        slot, group = r % 2, r // GROUP
        state = lax.rem(i, 2)
        for number, ch in enumerate(range(0, hid, CHUNK)):
            lines = [slice(g * hid + ch, g * hid + ch + CHUNK) for g in range(4)]
            bias = [bbuf[lines[g], :] for g in range(4)]
            totals = [None] * 4
            between[number]()
            for tile in range(TW):
                at = pl.ds(tile * hid * rows + ch * rows + r, CHUNK, stride=rows)
                c0, c1 = tile * cols, (tile + 1) * cols
                t_in, t_forget, t_out, cand = [
                    jnp.tanh(pre[slot, lines[g], c0:c1] + bias[g]) for g in range(4)
                ]
                in_gate = 0.5 * t_in + 0.5
                forget = 0.5 * t_forget + 0.5
                out_gate = 0.5 * t_out + 0.5
                before = cs[state, at, :]
                up = gs[state, at, :]
                now = forget * before + in_gate * cand
                squashed = jnp.tanh(now)
                hs[at, :] = out_gate * squashed
                ns[at, :] = now
                d_cell = up * out_gate * (1.0 - squashed * squashed)
                grads = (
                    d_cell * cand * (1.0 - t_in * t_in),
                    d_cell * before * (1.0 - t_forget * t_forget),
                    up * squashed * (1.0 - t_out * t_out),
                    d_cell * in_gate * (1.0 - cand * cand),
                )
                d0 = (r % GROUP) * span + c0
                for g in range(4):
                    gate[group % 2, lines[g], d0 : d0 + cols] = grads[g].astype(gate.dtype)
                    totals[g] = grads[g] if totals[g] is None else totals[g] + grads[g]
            for g in range(4):
                bias_acc[lines[g], :] += totals[g]

    load(cell, cv, c_sem, 0).wait()
    load(grad, gv, g_sem, 0).wait()
    for tile in range(TW):
        stage_state(0, 0, tile, 0, hid)
    for part in range(2):
        forward(0, 0, part)
    assert rows % (2 * GROUP) == 0 and GROUP == 2 and hid // CHUNK >= 4

    @pl.loop(0, bands)
    def _(i):
        following = jnp.minimum(i + 1, bands - 1)

        @pl.when(i + 1 < bands)
        def _():
            load(cell, cv, c_sem, i + 1).wait()
            load(grad, gv, g_sem, i + 1).wait()

        for r in range(rows):
            line = i * rows + r
            earlier = jnp.maximum(i * rows + (r // GROUP - 1) * GROUP, 0)
            share = hid * TW // rows
            tile, c0 = r * share // hid, r * share % hid

            def last(tile=tile, c0=c0):
                stage_state(following, i + 1, tile, c0, c0 + share)

            between = [
                functools.partial(forward, line + 1, (r + 1) % 2, 0),
                functools.partial(forward, line + 1, (r + 1) % 2, 1),
                functools.partial(backward, earlier, (r // GROUP - 1) % 2, r % GROUP),
                last,
            ] + [lambda: None] * (hid // CHUNK)
            pointwise(i, r, between)
        for tile in range(TW):
            live = flags[0, base_tile + i * TW + tile] >= 0
            lines = pl.ds(tile * hid * rows, hid * rows)
            where = i * TW + tile
            keep = jnp.where(live, 1.0, 0.0).astype(jnp.float32)
            alive = jnp.full((hid, rows, cols), keep) > 0.5
            ho[where] = jnp.where(
                alive, hs[lines].reshape(hid, rows, cols), hv[where].astype(jnp.float32)
            ).astype(ho.dtype)
            co[where] = jnp.where(
                alive, ns[lines].reshape(hid, rows, cols), cv[where].astype(jnp.float32)
            ).astype(co.dtype)
        store(ho, hidden_out, ho_sem, i).start()
        store(co, cell_out, co_sem, i).start()

    for part in range(2):
        backward(bands * rows - GROUP, (rows // GROUP - 1) % 2, part)
    quarter = jnp.where(row < 3 * hid, 0.25, 1.0).astype(jnp.float32)
    bias_sum = jnp.sum(bias_acc[...], axis=1, keepdims=True) * quarter
    column = lax.broadcasted_iota(jnp.int32, (gates, padded), 1)
    done = jnp.where(
        column < depth, acc[...].T * quarter, jnp.where(column == depth, bias_sum, 0.0)
    )
    if len(sums.shape) == 2:
        sums[...] = done
    else:
        n_dp, n_space = sums.shape[:2]
        sub, wide = gates // (n_dp * n_space), padded // 2
        for d in range(n_dp):
            for s in range(n_space):
                top = (s * n_dp + d) * sub
                sums[d, s] = jnp.concatenate(
                    [done[top : top + sub, 0:wide], done[top : top + sub, wide:]], axis=0
                ).astype(sums.dtype)
    put_sums.start()
    put_sums.wait()
    for i in range(bands):
        store(ho, hidden_out, ho_sem, i).wait()
        store(co, cell_out, co_sem, i).wait()


def run_step(sums, flags, halo, forcing, hidden, cell, grad, w_gates, gate_bias):
    _, tiles, in_ch, rows, cols = forcing.shape
    hid = hidden.shape[2]
    width = in_ch + hid
    bands = tiles // TW
    span = TW * cols
    depth, gates = w_gates.shape
    padded = -(-(depth + 1) // 256) * 256
    state = (tiles, hid, rows, cols)
    flat = (TW * hid * rows, cols)
    whole = pl.BlockSpec(memory_space=pl.ANY)
    vmem = pl.BlockSpec(memory_space=pltpu.VMEM)
    return pl.pallas_call(
        step_kernel,
        out_shape=(
            jax.ShapeDtypeStruct(hidden.shape, hidden.dtype),
            jax.ShapeDtypeStruct(cell.shape, cell.dtype),
            sums,
        ),
        in_specs=[pl.BlockSpec(memory_space=pltpu.SMEM), whole, whole, whole, whole, whole, whole, vmem],
        out_specs=(whole, whole, whole),
        scratch_shapes=[
            pltpu.VMEM((tiles, in_ch, rows, cols), jnp.bfloat16),
            pltpu.VMEM(state, jnp.bfloat16),
            pltpu.VMEM(state, jnp.bfloat16),
            pltpu.VMEM(state, jnp.bfloat16),
            pltpu.VMEM(state, jnp.bfloat16),
            pltpu.VMEM(state, jnp.bfloat16),
            pltpu.VMEM(((bands * rows + 3) * 3 * width + padded - depth, span), jnp.bfloat16),
            pltpu.VMEM((TW * width * rows, cols), jnp.float32),
            pltpu.VMEM((2,) + flat, jnp.float32),
            pltpu.VMEM((2,) + flat, jnp.float32),
            pltpu.VMEM(flat, jnp.float32),
            pltpu.VMEM(flat, jnp.float32),
            pltpu.VMEM((gates, padded), jnp.bfloat16),
            pltpu.VMEM((gates, cols), jnp.float32),
            pltpu.VMEM((2, gates, span), jnp.float32),
            pltpu.VMEM((2, gates, GROUP * span), jnp.bfloat16),
            pltpu.VMEM((gates, cols), jnp.float32),
            pltpu.VMEM(halo.shape, halo.dtype),
            pltpu.VMEM((padded, gates), jnp.bfloat16),
            pltpu.VMEM((padded, gates), jnp.float32),
            pltpu.VMEM(sums.shape, sums.dtype),
        ]
        + [pltpu.SemaphoreType.DMA((bands,))] * 6
        + [pltpu.SemaphoreType.DMA((3,))],
        compiler_params=pltpu.CompilerParams(vmem_limit_bytes=60 * 1024 * 1024),
        cost_estimate=pl.CostEstimate(
            flops=4 * gates * depth * tiles * rows * cols,
            bytes_accessed=12 * tiles * hid * rows * cols,
            transcendentals=5 * tiles * hid * rows * cols,
        ),
        name="step",
    )(flags, halo, forcing, hidden, cell, grad, w_gates, gate_bias)


def reduce_kernel(n_space, n_dp, sums, out, mine, first, second, part, third, own, s1, r1, s2, r2, s3, r3):
    sub = out.shape[0] // n_dp
    wide = sums.shape[-1]
    home, year = lax.axis_index("space"), lax.axis_index("dp")

    def years_off(off):
        return lax.rem(year + off, n_dp)

    def homes_off(off):
        return lax.rem(home + off, n_space)

    def over_years(off, place):
        return pltpu.make_async_remote_copy(
            src_ref=sums.at[years_off(off), homes_off(place)], dst_ref=first.at[off - 1, place],
            send_sem=s1.at[off - 1, place], recv_sem=r1.at[off - 1, place],
            device_id={"dp": years_off(off)}, device_id_type=MESH,
        )

    def over_homes(off):
        return pltpu.make_async_remote_copy(
            src_ref=part.at[off], dst_ref=second.at[off - 1], send_sem=s2.at[off - 1],
            recv_sem=r2.at[off - 1], device_id={"space": homes_off(off)}, device_id_type=MESH,
        )

    def to_years(off):
        return pltpu.make_async_remote_copy(
            src_ref=third.at[0], dst_ref=third.at[off], send_sem=s3.at[off - 1],
            recv_sem=r3.at[off - 1], device_id={"dp": years_off(off)}, device_id_type=MESH,
        )

    barrier = pltpu.get_barrier_semaphore()
    for off in range(1, n_dp):
        pl.semaphore_signal(barrier, inc=1, device_id={"dp": years_off(off)}, device_id_type=MESH)
    for off in range(1, n_space):
        pl.semaphore_signal(barrier, inc=1, device_id={"space": homes_off(off)}, device_id_type=MESH)
    get_mine = pltpu.make_async_copy(sums.at[year], mine, own)
    get_mine.start()
    pl.semaphore_wait(barrier, n_dp + n_space - 2)

    order = list(range(1, n_space)) + [0]
    for place in order:
        for off in range(1, n_dp):
            over_years(off, place).start()
    get_mine.wait()
    for place in order:
        total = mine[homes_off(place)].astype(jnp.float32)
        for off in range(1, n_dp):
            over_years(off, place).wait_recv()
            total = total + first[off - 1, place].astype(jnp.float32)
        if place:
            part[place] = total.astype(part.dtype)
            over_homes(place).start()
    for off in range(1, n_space):
        over_homes(off).wait_recv()
        total = total + second[off - 1].astype(jnp.float32)
    third[0] = total
    for off in range(1, n_dp):
        to_years(off).start()
    for off in range(n_dp):
        if off:
            to_years(off).wait_recv()
        whose = lax.rem(year - off + n_dp, n_dp)
        lines = pl.ds(pl.multiple_of(whose * sub, 8), sub)
        out[lines, 0:wide] = third[off, 0:sub, :]
        out[lines, wide:] = third[off, sub:, :]
    for place in order:
        for off in range(1, n_dp):
            over_years(off, place).wait_send()
    for off in range(1, n_space):
        over_homes(off).wait_send()
    for off in range(1, n_dp):
        to_years(off).wait_send()


def reduce_all(sums, gates):
    n_dp, n_space, _, wide = sums.shape
    keep = gates // n_space
    block = sums.shape[2:]
    return pl.pallas_call(
        functools.partial(reduce_kernel, n_space, n_dp),
        out_shape=jax.ShapeDtypeStruct((keep, 2 * wide), jnp.float32),
        in_specs=[pl.BlockSpec(memory_space=pl.ANY)],
        out_specs=pl.BlockSpec(memory_space=pltpu.VMEM),
        scratch_shapes=[
            pltpu.VMEM((n_space,) + block, jnp.bfloat16),
            pltpu.VMEM((n_dp - 1, n_space) + block, jnp.bfloat16),
            pltpu.VMEM((n_space - 1,) + block, jnp.bfloat16),
            pltpu.VMEM((n_space,) + block, jnp.bfloat16),
            pltpu.VMEM((n_dp,) + block, jnp.float32),
            pltpu.SemaphoreType.DMA,
            pltpu.SemaphoreType.DMA((n_dp - 1, n_space)),
            pltpu.SemaphoreType.DMA((n_dp - 1, n_space)),
            pltpu.SemaphoreType.DMA((n_space - 1,)),
            pltpu.SemaphoreType.DMA((n_space - 1,)),
            pltpu.SemaphoreType.DMA((n_dp - 1,)),
            pltpu.SemaphoreType.DMA((n_dp - 1,)),
        ],
        compiler_params=pltpu.CompilerParams(collective_id=1, has_side_effects=True),
        name="reduce",
    )(sums)


def shards(n_space, n_dp, forcing, hidden_prev, cell_prev, hidden_grad, w_gates, gate_bias, worker):
    gates, depth = w_gates.shape
    halo = exchange_halo(forcing, hidden_prev, n_space)
    padded = -(-(depth + 1) // 256) * 256
    sub, ragged = divmod(gates, n_space * n_dp)
    staged = ragged == 0 and sub % 8 == 0
    sums = jax.ShapeDtypeStruct((gates, padded), jnp.float32)
    if staged:
        sums = jax.ShapeDtypeStruct((n_dp, n_space, 2 * sub, padded // 2), jnp.bfloat16)
    hidden_next, cell_next, sums = run_step(
        sums, worker, halo, forcing, hidden_prev, cell_prev, hidden_grad, w_gates.T, gate_bias[None, :]
    )
    if staged:
        total = reduce_all(sums, gates)
    else:
        total = lax.psum(lax.psum_scatter(sums, "space", scatter_dimension=0, tiled=True), "dp")
    return hidden_next, cell_next, total[:, :depth], total[:, depth]


def solution(mesh):
    state = P("dp", "space", None, None, None)
    return jax.shard_map(
        functools.partial(shards, mesh.shape["space"], mesh.shape["dp"]),
        mesh=mesh,
        in_specs=(state, state, state, state, P(), P(), P("dp", None)),
        out_specs=(state, state, P("space", None), P("space")),
        check_vma=False,
    )
```
